32 devices in a mesh: grp: 2 (over x), space: 16 (over z, y, core).
Axes of the slice: x: 2, y: 2, z: 4, core: 2. Of those that a mesh axis runs over, the one named last changes fastest.
Arguments:
- right_side: float32 [64, 32, 4096], P(None, None, ('grp', 'space')), parts along dimension 2, may hold values from -36 to 36
- diag_tiles: bfloat16 [64, 64, 4096], P(None, None, ('grp', 'space')), parts along dimension 2, may hold values from -0.5 to 4.5, as said below
- off_tiles: bfloat16 [15, 64, 64, 4096], P(None, None, None, ('grp', 'space')), parts along dimension 3, may hold values from -0.1875 to 0.1875
- neighbours: int32 [15, 4096], P(None, ('grp', 'space')), parts along dimension 1, may hold values from -192 to 2046, as said below
Outputs:
- solution: float32 [64, 32, 4096], P(None, None, ('grp', 'space')), parts along dimension 2
- residual: float32 [64, 32, 4096], P(None, None, ('grp', 'space')), parts along dimension 2
The draws below stay inside these ranges and needn't reach their ends.
There are 2 independent parts, one for each index of `grp`. The reference program is written for one: setup_inputs(seed, part) draws one part's arguments, and reference() takes and returns one part's arrays. A program takes and returns all parts, laid end to end along the dimension named above; each array names one. Nothing has to cross between parts.
Inputs may be any that keep to these rules, and one draw needn't show every extreme that they name: `neighbours`: the 15 ids of one block i differ and lie from i - 192 to i - 1; ids below 0 name no block and add nothing. `diag_tiles`: diagonal tiles have positive diagonals of 1.2 to 4 and smaller entries off them.
All inputs are finite; a program needn't handle non-finite values.
Results may differ from the reference program's by a relative error of at most 0.0068.
Values may be sent and summed in bfloat16 or wider, within the bound.
A program may use at most 192 MiB of HBM per device.

```python
import jax
import jax.numpy as jnp
from jax import lax

BLK = 64
RHS = 32
NNB = 15
NB_DEV = 128
NBLK = 2048


def draw_right_side(key, part):
    key = jax.random.fold_in(key, 11)
    first, second = jax.random.split(key)
    position = jnp.arange(NBLK, dtype=jnp.float32) / max(NBLK - 1, 1)
    base = jnp.clip(jax.random.normal(first, (BLK, RHS, NBLK), jnp.float32), -4.0, 4.0)
    slope = 0.5
    ramp = jnp.exp(jnp.log(3.0) * slope * position)
    spread = jnp.exp(jax.random.uniform(second, (1, RHS, NBLK), jnp.float32) * jnp.log(10.0))
    return (0.3 * base * spread * ramp[None, None, :]).astype(jnp.float32)


def draw_diag_tiles(key, part):
    key = jax.random.fold_in(key, 17)
    first, second = jax.random.split(key)
    eye_mask = jnp.eye(BLK, dtype=jnp.float32)[:, :, None]
    main = jax.random.uniform(first, (1, BLK, NBLK), jnp.float32, 1.5, 3.0)
    rough = 0.08 * jnp.clip(jax.random.normal(second, (BLK, BLK, NBLK), jnp.float32), -5.0, 5.0)
    tiles = eye_mask * main + (1.0 - eye_mask) * rough
    return tiles.astype(jnp.bfloat16)


def draw_neighbours(key, part):
    key = jax.random.fold_in(key, 23)
    reach = 3 * NB_DEV // 2
    scores = jax.random.randint(key, (NBLK, reach), 0, 1 << 20) * reach + jnp.arange(reach, dtype=jnp.int32)[None, :]
    picked = lax.top_k(scores, NNB)[1].astype(jnp.int32)
    ids = jnp.arange(NBLK, dtype=jnp.int32)[:, None] - 1 - picked
    return ids.T.astype(jnp.int32)


def block_scale(key, shape, pieces, least, top_value):
    gain = 1.0
    for dim, shards_of in pieces:
        draws = jax.random.uniform(jax.random.fold_in(jax.random.fold_in(key, 6), dim), (shards_of,), jnp.float32, least / len(pieces), top_value / len(pieces))
        gain = gain * jnp.repeat(jnp.exp(draws), shape[dim] // shards_of).reshape((-1,) + (1,) * (len(shape) - 1 - dim))
    return gain


def noise(own_key, dims, deviation, limit, shards=(), kind=jnp.bfloat16):
    loudness = block_scale(own_key, dims, shards, -0.22, 0.18) if shards else 1.0
    values = jax.random.normal(own_key, dims, jnp.float32) * deviation * loudness
    return jnp.minimum(jnp.maximum(values, -limit), limit).astype(kind)


def setup_inputs(seed: int = 0, part: int = 0) -> dict:
    keys = jax.random.split(jax.random.key(seed), 5)
    part_splits = jax.random.split(jax.random.fold_in(keys[4], part), 5)
    return {
        "right_side": draw_right_side(jax.random.fold_in(jax.random.fold_in(keys[4], part), 71), part),
        "diag_tiles": draw_diag_tiles(jax.random.fold_in(jax.random.fold_in(keys[4], part), 71), part),
        "off_tiles": noise(part_splits[2], (NNB, BLK, BLK, NBLK), (BLK * NNB) ** -0.5, 0.1875, ((3, 16),)),
        "neighbours": draw_neighbours(jax.random.fold_in(jax.random.fold_in(keys[4], part), 71), part),
    }


def reference(right_side, diag_tiles, off_tiles, neighbours):
    highest = lax.Precision.HIGHEST
    rounded = right_side.astype(jnp.bfloat16).astype(jnp.float32)
    diagonal = diag_tiles.astype(jnp.float32)
    image = jnp.einsum("lki,kri->lri", diagonal, rounded, precision=highest)
    for slot in range(NNB):
        column = neighbours[slot]
        usable = (column >= 0).astype(jnp.float32)
        safe_ids = jnp.maximum(column, 0).astype(jnp.int32)
        gathered = rounded[:, :, safe_ids] * usable[None, None, :]
        coupling = off_tiles[slot].astype(jnp.float32)
        image = image + jnp.einsum("lki,kri->lri", coupling, gathered, precision=highest)
    image_rounded = image.astype(jnp.bfloat16).astype(jnp.float32)
    product = jnp.einsum("kli,kri->lri", diagonal, image_rounded, precision=highest)
    for slot in range(NNB):
        column = neighbours[slot]
        usable = (column >= 0).astype(jnp.float32)
        safe_ids = jnp.maximum(column, 0).astype(jnp.int32)
        coupling = off_tiles[slot].astype(jnp.float32)
        terms = jnp.einsum("lki,lri->kri", coupling, image_rounded, precision=highest)
        product = product.at[:, :, safe_ids].add(terms * usable[None, None, :])
    norm = jnp.sum(right_side * right_side, axis=(0, 2))
    curve = jnp.sum(image * image_rounded, axis=(0, 2))
    step_size = (norm / curve)[None, :, None]
    solution = step_size * right_side
    residual = right_side - step_size * product
    return solution, residual
```

```python
import functools

import jax
import jax.numpy as jnp
from jax import lax
from jax.experimental import pallas as pl
from jax.experimental.pallas import tpu as pltpu
from jax.sharding import PartitionSpec as P

GROUP = 8


def from_behind(value, axis, steps):
    count = lax.axis_size(axis)
    first, last = (max(0, -steps), min(count, count - steps))
    return lax.ppermute(value, axis, [(source, source + steps) for source in range(first, last)])


def turn_kernel(off_ref, diag_ref, out_ref):
    slots, rows, depth, blocks = off_ref.shape
    groups = blocks // GROUP
    for pair in range(rows // 2):
        for m in range((slots + 1) // 2):
            parts = []
            for row in (2 * pair, 2 * pair + 1):
                first = off_ref[2 * m, row]
                second = off_ref[2 * m + 1, row] if 2 * m + 1 < slots else diag_ref[row]
                both = jnp.concatenate([first, second], axis=0).astype(jnp.float32)
                parts.append(both.T.reshape(groups, GROUP, 2 * depth))
            packed = jnp.concatenate(parts, axis=1).astype(jnp.bfloat16)
            out_ref[:, pair * 16 : pair * 16 + 16, m * 2 * depth : (m + 1) * 2 * depth] = packed


def turn_tiles(off_tiles, diag_tiles):
    slots, rows, depth, blocks = off_tiles.shape
    step = 8
    groups = blocks // GROUP
    wide = (slots + 1) * depth
    return pl.pallas_call(
        turn_kernel,
        grid=(rows // step,),
        in_specs=[
            pl.BlockSpec((slots, step, depth, blocks), lambda s: (0, s, 0, 0)),
            pl.BlockSpec((step, depth, blocks), lambda s: (s, 0, 0)),
        ],
        out_specs=pl.BlockSpec((groups, step * GROUP, wide), lambda s: (0, s, 0)),
        out_shape=jax.ShapeDtypeStruct((groups, rows * GROUP, wide), jnp.bfloat16),
        compiler_params=pltpu.CompilerParams(vmem_limit_bytes=40 * 2**20),
        cost_estimate=pl.CostEstimate(flops=0, bytes_accessed=64 * 2**20, transcendentals=0),
        name="turn_tiles",
    )(off_tiles, diag_tiles)


def low_lanes(shape):
    return lax.broadcasted_iota(jnp.int32, shape, len(shape) - 1) < shape[-1] // 2


def main_kernel(
    ids_ref, own_ref, earlier_ref, oldest_ref, t_ref,
    for_oldest_ref, for_earlier_ref, own_out_ref, curve_ref,
    low_table, high_table, low_sum, high_sum, picked, terms,
):
    step = pl.program_id(0)
    half = own_ref.shape[0]
    quarter = oldest_ref.shape[0]
    rhs, lanes = own_ref.shape[1:]
    depth = lanes // 2
    pairs = t_ref.shape[2] // lanes
    starts = (0, 2 * quarter, 2 * quarter + 2 * half)

    @pl.when(step == 0)
    def _():
        low = low_lanes((rhs, lanes))
        for source, start in zip((oldest_ref, earlier_ref, own_ref), starts):
            size = source.shape[0]

            @pl.loop(0, size)
            def _(j):
                page = source[j].astype(jnp.float32)
                other = pltpu.roll(page, depth, 1)
                for table, here in ((low_table, low), (high_table, ~low)):
                    first, second = (page, other) if table is low_table else (other, page)
                    table[start + j] = jnp.where(here, first, 0.0).astype(jnp.bfloat16)
                    table[start + size + j] = jnp.where(here, second, 0.0).astype(jnp.bfloat16)

        @pl.loop(0, low_sum.shape[0])
        def _(j):
            low_sum[j] = jnp.zeros((rhs, lanes), jnp.float32)
            high_sum[j] = jnp.zeros((rhs, lanes), jnp.float32)

        curve_ref[...] = jnp.zeros_like(curve_ref)

    for b in range(GROUP):
        for m in range(pairs):
            first = ids_ref[2 * m, step * GROUP + b]
            second = ids_ref[2 * m + 1, step * GROUP + b]
            picked[b * rhs : (b + 1) * rhs, m * lanes : (m + 1) * lanes] = low_table[first] + high_table[second]

    image = lax.dot_general(
        t_ref[0], picked[...], (((1,), (1,)), ((), ())), preferred_element_type=jnp.float32
    )
    row = lax.broadcasted_iota(jnp.int32, image.shape, 0) % GROUP
    column = lax.broadcasted_iota(jnp.int32, image.shape, 1) // rhs
    image = jnp.where(row == column, image, 0.0)
    rounded = image.astype(jnp.bfloat16)
    curve_ref[...] += jnp.sum(image * rounded.astype(jnp.float32), axis=0, keepdims=True)
    terms[...] = lax.dot_general(
        rounded, t_ref[0], (((0,), (0,)), ((), ())), preferred_element_type=jnp.float32
    )
    for b in range(GROUP):
        for table, odd in ((low_sum, 0), (high_sum, 1)):
            for begin in range(0, pairs, 4):
                ids = [ids_ref[2 * m + odd, step * GROUP + b] for m in range(begin, begin + 4)]
                sums = [
                    table[ids[m - begin]] + terms[b * rhs : (b + 1) * rhs, m * lanes : (m + 1) * lanes]
                    for m in range(begin, begin + 4)
                ]
                for at, value in zip(ids, sums):
                    table[at] = value

    @pl.when(step == pl.num_programs(0) - 1)
    def _():
        low = low_lanes((rhs, lanes))

        def total(t):
            mixed = jnp.where(low, low_sum[t], high_sum[t])
            return mixed + pltpu.roll(mixed, depth, 1)

        for out, start in zip((for_oldest_ref, for_earlier_ref, own_out_ref), starts):
            size = out.shape[0]

            @pl.loop(0, size)
            def _(j):
                out[j] = jnp.where(low, total(start + j), total(start + size + j)).astype(out.dtype)


def main_call(ids, own, earlier, oldest, turned):
    half, rhs, lanes = own.shape
    quarter = oldest.shape[0]
    groups, rows, wide = turned.shape
    pages = 4 * half + 2 * quarter
    whole = lambda shape: pl.BlockSpec(shape, lambda s: (0,) * len(shape))
    return pl.pallas_call(
        main_kernel,
        grid=(groups,),
        in_specs=[
            pl.BlockSpec(memory_space=pltpu.SMEM),
            whole(own.shape),
            whole(earlier.shape),
            whole(oldest.shape),
            pl.BlockSpec((1, rows, wide), lambda s: (s, 0, 0)),
        ],
        out_specs=[whole(oldest.shape), whole(own.shape), whole(own.shape), whole((1, GROUP * rhs))],
        out_shape=[
            jax.ShapeDtypeStruct(oldest.shape, jnp.bfloat16),
            jax.ShapeDtypeStruct(own.shape, jnp.bfloat16),
            jax.ShapeDtypeStruct(own.shape, jnp.float32),
            jax.ShapeDtypeStruct((1, GROUP * rhs), jnp.float32),
        ],
        scratch_shapes=[
            pltpu.VMEM((pages, rhs, lanes), jnp.bfloat16),
            pltpu.VMEM((pages, rhs, lanes), jnp.bfloat16),
            pltpu.VMEM((pages, rhs, lanes), jnp.float32),
            pltpu.VMEM((pages, rhs, lanes), jnp.float32),
            pltpu.VMEM((GROUP * rhs, wide), jnp.bfloat16),
            pltpu.VMEM((GROUP * rhs, wide), jnp.float32),
        ],
        compiler_params=pltpu.CompilerParams(vmem_limit_bytes=48 * 2**20),
        cost_estimate=pl.CostEstimate(flops=8 * 10**9, bytes_accessed=32 * 2**20, transcendentals=0),
        name="image_and_terms",
    )(ids, own, earlier, oldest, turned)


def on_device(right_side, diag_tiles, off_tiles, neighbours):
    depth, rhs, blocks = right_side.shape
    half = blocks // 2
    quarter = half // 2
    device = lax.axis_index("space")
    own = (
        right_side.astype(jnp.bfloat16)
        .reshape(depth, rhs, 2, half)
        .transpose(3, 1, 2, 0)
        .reshape(half, rhs, 2 * depth)
    )
    late = own[:, :, depth:]
    late = jnp.concatenate([late[:quarter], late[quarter:]], axis=2)
    earlier = from_behind(own, "space", 1)
    oldest = from_behind(late, "space", 2)
    turned = turn_tiles(off_tiles, diag_tiles)
    ids = jnp.concatenate(
        [
            neighbours - (device * blocks - blocks - half),
            (blocks + half + jnp.arange(blocks, dtype=jnp.int32))[None],
        ],
        axis=0,
    )
    for_oldest, for_earlier, own_sum, curve_parts = main_call(ids, own, earlier, oldest, turned)
    from_next = from_behind(for_earlier, "space", -1).astype(jnp.float32)
    from_after = from_behind(for_oldest, "space", -2).astype(jnp.float32)
    norm_local = jnp.sum(right_side * right_side, axis=(0, 2))
    curve_local = jnp.sum(curve_parts.reshape(GROUP, rhs), axis=0)
    norm, curve = lax.psum(jnp.stack([norm_local, curve_local]), "space")
    after = jnp.concatenate([from_after[:, :, :depth], from_after[:, :, depth:]], axis=0)
    product = own_sum + from_next + jnp.pad(after, ((0, 0), (0, 0), (depth, 0)))
    product = product.reshape(half, rhs, 2, depth).transpose(3, 1, 2, 0).reshape(depth, rhs, blocks)
    step_size = (norm / curve)[None, :, None]
    solution = step_size * right_side
    residual = right_side - step_size * product
    return (solution, residual)


def solution(mesh):
    placed = (
        P(None, None, ("grp", "space")),
        P(None, None, ("grp", "space")),
        P(None, None, None, ("grp", "space")),
        P(None, ("grp", "space")),
    )
    return jax.shard_map(
        on_device,
        mesh=mesh,
        in_specs=placed,
        out_specs=(P(None, None, ("grp", "space")), P(None, None, ("grp", "space"))),
        check_vma=False,
    )
```

```python
import functools

import jax
import jax.numpy as jnp
from jax import lax
from jax.experimental import pallas as pl
from jax.experimental.pallas import tpu as pltpu
from jax.sharding import PartitionSpec as P

GROUP = 8


def from_behind(value, axis, steps):
    count = lax.axis_size(axis)
    first, last = (max(0, -steps), min(count, count - steps))
    return lax.ppermute(value, axis, [(source, source + steps) for source in range(first, last)])


def turn_kernel(off_ref, diag_ref, out_ref):
    slots, rows, depth, blocks = off_ref.shape
    groups = blocks // GROUP
    for pair in range(rows // 2):
        for m in range((slots + 1) // 2):
            parts = []
            for row in (2 * pair, 2 * pair + 1):
                first = off_ref[2 * m, row]
                second = off_ref[2 * m + 1, row] if 2 * m + 1 < slots else diag_ref[row]
                both = jnp.concatenate([first, second], axis=0).astype(jnp.float32)
                parts.append(both.T.reshape(groups, GROUP, 2 * depth))
            packed = jnp.concatenate(parts, axis=1).astype(jnp.bfloat16)
            out_ref[:, pair * 16 : pair * 16 + 16, m * 2 * depth : (m + 1) * 2 * depth] = packed


def turn_tiles(off_tiles, diag_tiles):
    slots, rows, depth, blocks = off_tiles.shape
    step = 8
    groups = blocks // GROUP
    wide = (slots + 1) * depth
    return pl.pallas_call(
        turn_kernel,
        grid=(rows // step,),
        in_specs=[
            pl.BlockSpec((slots, step, depth, blocks), lambda s: (0, s, 0, 0)),
            pl.BlockSpec((step, depth, blocks), lambda s: (s, 0, 0)),
        ],
        out_specs=pl.BlockSpec((groups, step * GROUP, wide), lambda s: (0, s, 0)),
        out_shape=jax.ShapeDtypeStruct((groups, rows * GROUP, wide), jnp.bfloat16),
        compiler_params=pltpu.CompilerParams(vmem_limit_bytes=40 * 2**20),
        cost_estimate=pl.CostEstimate(flops=0, bytes_accessed=64 * 2**20, transcendentals=0),
        name="turn_tiles",
    )(off_tiles, diag_tiles)


def low_lanes(shape):
    return lax.broadcasted_iota(jnp.int32, shape, len(shape) - 1) < shape[-1] // 2


def main_kernel(
    ids_ref, own_ref, earlier_ref, oldest_ref, t_ref,
    for_oldest_ref, for_earlier_ref, own_out_ref, curve_ref,
    low_table, high_table, low_sum, high_sum, picked, terms,
):
    step = pl.program_id(0)
    half = own_ref.shape[0]
    quarter = oldest_ref.shape[0]
    rhs, lanes = own_ref.shape[1:]
    depth = lanes // 2
    pairs = t_ref.shape[2] // lanes
    starts = (0, 2 * quarter, 2 * quarter + 2 * half)
    base = lax.axis_index("space") * (2 * half) - starts[2]

    def page_of(slot, b):
        block = step * GROUP + b
        return starts[2] + block if slot == 2 * pairs - 1 else ids_ref[slot, block] - base

    @pl.when(step == 0)
    def _():
        low = low_lanes((rhs, lanes))
        for source, start in zip((oldest_ref, earlier_ref, own_ref), starts):
            size = source.shape[0]

            @pl.loop(0, size, unroll=8)
            def _(j):
                page = source[j].astype(jnp.float32)
                other = pltpu.roll(page, depth, 1)
                for table, here in ((low_table, low), (high_table, ~low)):
                    first, second = (page, other) if table is low_table else (other, page)
                    table[start + j] = jnp.where(here, first, 0.0).astype(jnp.bfloat16)
                    table[start + size + j] = jnp.where(here, second, 0.0).astype(jnp.bfloat16)

        @pl.loop(0, low_sum.shape[0], unroll=8)
        def _(j):
            low_sum[j] = jnp.zeros((rhs, lanes), jnp.float32)
            high_sum[j] = jnp.zeros((rhs, lanes), jnp.float32)

        curve_ref[...] = jnp.zeros_like(curve_ref)

    for b in range(GROUP):
        for m in range(pairs):
            first, second = page_of(2 * m, b), page_of(2 * m + 1, b)
            picked[b * rhs : (b + 1) * rhs, m * lanes : (m + 1) * lanes] = low_table[first] + high_table[second]

    image = lax.dot_general(
        t_ref[0], picked[...], (((1,), (1,)), ((), ())), preferred_element_type=jnp.float32
    )
    shape = (1, GROUP, image.shape[1])
    start = lax.broadcasted_iota(jnp.int32, shape, 1) * rhs
    column = lax.broadcasted_iota(jnp.int32, shape, 2)
    meant = (column >= start) & (column < start + rhs)
    image = jnp.where(meant, image.reshape(-1, GROUP, shape[2]), 0.0)
    rounded = image.reshape(-1, shape[2]).astype(jnp.bfloat16)
    square = image * rounded.astype(jnp.float32).reshape(image.shape)
    curve_ref[...] += jnp.sum(square, axis=0)
    terms[...] = lax.dot_general(
        rounded, t_ref[0], (((0,), (0,)), ((), ())), preferred_element_type=jnp.float32
    )
    for b in range(GROUP):
        for table, odd in ((low_sum, 0), (high_sum, 1)):
            for begin in range(0, pairs, 4):
                ids = [page_of(2 * m + odd, b) for m in range(begin, begin + 4)]
                sums = [
                    table[ids[m - begin]] + terms[b * rhs : (b + 1) * rhs, m * lanes : (m + 1) * lanes]
                    for m in range(begin, begin + 4)
                ]
                for at, value in zip(ids, sums):
                    table[at] = value

    @pl.when(step == pl.num_programs(0) - 1)
    def _():
        low = low_lanes((rhs, lanes))

        def total(t):
            mixed = jnp.where(low, low_sum[t], high_sum[t])
            return mixed + pltpu.roll(mixed, depth, 1)

        for out, start in zip((for_oldest_ref, for_earlier_ref, own_out_ref), starts):
            size = out.shape[0]

            @pl.loop(0, size, unroll=8)
            def _(j):
                out[j] = jnp.where(low, total(start + j), total(start + size + j)).astype(out.dtype)


def main_call(ids, own, earlier, oldest, turned):
    half, rhs, lanes = own.shape
    quarter = oldest.shape[0]
    groups, rows, wide = turned.shape
    pages = 4 * half + 2 * quarter
    whole = lambda shape: pl.BlockSpec(shape, lambda s: (0,) * len(shape))
    return pl.pallas_call(
        main_kernel,
        grid=(groups,),
        in_specs=[
            pl.BlockSpec(memory_space=pltpu.SMEM),
            whole(own.shape),
            whole(earlier.shape),
            whole(oldest.shape),
            pl.BlockSpec((1, rows, wide), lambda s: (s, 0, 0)),
        ],
        out_specs=[whole(oldest.shape), whole(own.shape), whole(own.shape), whole((GROUP, GROUP * rhs))],
        out_shape=[
            jax.ShapeDtypeStruct(oldest.shape, jnp.bfloat16),
            jax.ShapeDtypeStruct(own.shape, jnp.bfloat16),
            jax.ShapeDtypeStruct(own.shape, jnp.float32),
            jax.ShapeDtypeStruct((GROUP, GROUP * rhs), jnp.float32),
        ],
        scratch_shapes=[
            pltpu.VMEM((pages, rhs, lanes), jnp.bfloat16),
            pltpu.VMEM((pages, rhs, lanes), jnp.bfloat16),
            pltpu.VMEM((pages, rhs, lanes), jnp.float32),
            pltpu.VMEM((pages, rhs, lanes), jnp.float32),
            pltpu.VMEM((GROUP * rhs, wide), jnp.bfloat16),
            pltpu.VMEM((GROUP * rhs, wide), jnp.float32),
        ],
        compiler_params=pltpu.CompilerParams(vmem_limit_bytes=48 * 2**20),
        cost_estimate=pl.CostEstimate(flops=8 * 10**9, bytes_accessed=32 * 2**20, transcendentals=0),
        name="image_and_terms",
    )(ids, own, earlier, oldest, turned)


def prepare_kernel(x_ref, own_ref, late_ref, wide):
    half, rhs, lanes = own_ref.shape
    quarter = late_ref.shape[0]
    depth = lanes // 2
    for r in range(rhs):
        turned = x_ref[:, r, :].T
        wide[:, r, :] = jnp.concatenate([turned[:half], turned[half:]], axis=1)
    own_ref[...] = wide[...].astype(jnp.bfloat16)
    low = low_lanes((quarter, rhs, lanes))
    first = pltpu.roll(wide[:quarter], depth, 2)
    late_ref[...] = jnp.where(low, first, wide[quarter:]).astype(jnp.bfloat16)


def prepare(right_side):
    depth, rhs, blocks = right_side.shape
    half = blocks // 2
    return pl.pallas_call(
        prepare_kernel,
        out_shape=[
            jax.ShapeDtypeStruct((half, rhs, 2 * depth), jnp.bfloat16),
            jax.ShapeDtypeStruct((half // 2, rhs, 2 * depth), jnp.bfloat16),
        ],
        scratch_shapes=[pltpu.VMEM((half, rhs, 2 * depth), jnp.float32)],
        compiler_params=pltpu.CompilerParams(vmem_limit_bytes=24 * 2**20),
        name="prepare",
    )(right_side)


def finish_kernel(
    count, oldest_ref, earlier_ref, own_ref, curve_ref, x_ref, solution_ref, residual_ref,
    after, following, parts, part, turned, small_sent, small_got, sent, got,
):
    mesh_ids = pl.DeviceIdType.MESH
    me = lax.axis_index("space")
    depth, rhs, blocks = x_ref.shape
    half, _, lanes = own_ref.shape
    quarter = oldest_ref.shape[0]
    row = lax.broadcasted_iota(jnp.int32, (rhs, lanes), 0)
    lane = lax.broadcasted_iota(jnp.int32, (rhs, lanes), 1)
    diagonal = row == lane

    barrier = pltpu.get_barrier_semaphore()

    @pl.loop(1, count)
    def _(k):
        pl.semaphore_signal(
            barrier, inc=1, device_id={"space": lax.rem(me + k, count)}, device_id_type=mesh_ids
        )

    squares = jnp.zeros((rhs, blocks), jnp.float32)
    for k in range(depth):
        squares = squares + x_ref[k] * x_ref[k]
    norms = jnp.sum(squares, axis=1, keepdims=True)
    part[...] = jnp.zeros_like(part)
    part[0:1, :] = jnp.sum(jnp.where(diagonal, norms, 0.0), axis=0, keepdims=True)
    curves = jnp.sum(curve_ref[...], axis=0, keepdims=True)
    curves = curves[:, :lanes] + curves[:, lanes:]
    folded = curves
    for turn in range(rhs, lanes, rhs):
        folded = folded + pltpu.roll(curves, turn, 1)
    part[1:2, :] = folded

    pl.semaphore_wait(barrier, count - 1)

    def small(k, slot):
        return pltpu.make_async_remote_copy(
            src_ref=part,
            dst_ref=parts.at[slot],
            send_sem=small_sent.at[k],
            recv_sem=small_got.at[slot],
            device_id={"space": lax.rem(me + k, count)},
            device_id_type=mesh_ids,
        )

    @pl.loop(1, count)
    def _(k):
        small(k, me).start()

    def behind(source, landing, steps):
        return pltpu.make_async_remote_copy(
            src_ref=source,
            dst_ref=landing,
            send_sem=sent.at[steps - 1],
            recv_sem=got.at[steps - 1],
            device_id={"space": lax.rem(me + count - steps, count)},
            device_id_type=mesh_ids,
        )

    moves = (behind(earlier_ref, following, 1), behind(oldest_ref, after, 2))
    for steps, move in enumerate(moves, 1):

        @pl.when(me >= steps)
        def _():
            move.start()

    parts[me] = part[...]

    @pl.loop(1, count)
    def _(k):
        small(k, lax.rem(me + k, count)).wait_recv()

    total = parts[0]
    for slot in range(1, count):
        total = total + parts[slot]
    ratio = total[0:1, :] / total[1:2, :]
    scale = jnp.sum(jnp.where(diagonal, ratio, 0.0), axis=1, keepdims=True)
    for k in range(depth):
        solution_ref[k] = scale * x_ref[k]

    for steps, (move, landing) in enumerate(zip(moves, (following, after)), 1):

        @pl.when(me < count - steps)
        def _():
            move.wait_recv()

        @pl.when(me >= count - steps)
        def _():
            landing[...] = jnp.zeros_like(landing)

    low = low_lanes((rhs, lanes))
    for j in range(quarter):
        page = after[j].astype(jnp.float32)
        own_ref_low = jnp.where(low, 0.0, pltpu.roll(page, depth, 1))
        turned[j] = own_ref[j] + following[j].astype(jnp.float32) + own_ref_low
        at = quarter + j
        turned[at] = own_ref[at] + following[at].astype(jnp.float32) + jnp.where(low, 0.0, page)
    for r in range(rhs):
        side = turned[:, r, :].T
        side = jnp.concatenate([side[:depth], side[depth:]], axis=1)
        residual_ref[:, r, :] = x_ref[:, r, :] - scale[r : r + 1] * side

    @pl.loop(1, count)
    def _(k):
        small(k, me).wait_send()

    for steps, move in enumerate(moves, 1):

        @pl.when(me >= steps)
        def _():
            move.wait_send()


def finish(count, for_oldest, for_earlier, own_sum, curve_parts, right_side):
    vmem = pl.BlockSpec(memory_space=pltpu.VMEM)
    return pl.pallas_call(
        functools.partial(finish_kernel, count),
        in_specs=[vmem] * 5,
        out_specs=[vmem] * 2,
        out_shape=[jax.ShapeDtypeStruct(right_side.shape, jnp.float32)] * 2,
        scratch_shapes=[
            pltpu.VMEM(for_oldest.shape, jnp.bfloat16),
            pltpu.VMEM(for_earlier.shape, jnp.bfloat16),
            pltpu.VMEM((count, 8, own_sum.shape[2]), jnp.float32),
            pltpu.VMEM((8, own_sum.shape[2]), jnp.float32),
            pltpu.VMEM(own_sum.shape, jnp.float32),
            pltpu.SemaphoreType.DMA((count,)),
            pltpu.SemaphoreType.DMA((count,)),
            pltpu.SemaphoreType.DMA((2,)),
            pltpu.SemaphoreType.DMA((2,)),
        ],
        compiler_params=pltpu.CompilerParams(
            collective_id=0, has_side_effects=True, vmem_limit_bytes=24 * 2**20
        ),
        name="finish",
    )(for_oldest, for_earlier, own_sum, curve_parts, right_side)


def on_device(count, right_side, diag_tiles, off_tiles, neighbours):
    own, late = prepare(right_side)
    earlier = from_behind(own, "space", 1)
    oldest = from_behind(late, "space", 2)
    turned = turn_tiles(off_tiles, diag_tiles)
    for_oldest, for_earlier, own_sum, curve_parts = main_call(neighbours, own, earlier, oldest, turned)
    return tuple(finish(count, for_oldest, for_earlier, own_sum, curve_parts, right_side))


def solution(mesh):
    placed = (
        P(None, None, ("grp", "space")),
        P(None, None, ("grp", "space")),
        P(None, None, None, ("grp", "space")),
        P(None, ("grp", "space")),
    )
    return jax.shard_map(
        functools.partial(on_device, mesh.shape["space"]),
        mesh=mesh,
        in_specs=placed,
        out_specs=(P(None, None, ("grp", "space")), P(None, None, ("grp", "space"))),
        check_vma=False,
    )
```

```python
import functools

import jax
import jax.numpy as jnp
from jax import lax
from jax.experimental import pallas as pl
from jax.experimental.pallas import tpu as pltpu
from jax.sharding import PartitionSpec as P

GROUP = 8
TOGETHER = 2
TURN_MIB = 40
MAIN_MIB = 40


def low_lanes(shape):
    return lax.broadcasted_iota(jnp.int32, shape, len(shape) - 1) < shape[-1] // 2


def turn_kernel(
    count, x_ref, off_ref, diag_ref, own_ref, earlier_ref, oldest_ref, out_ref,
    wide, own, late, following, after, sent, got,
):
    mesh_ids = pl.DeviceIdType.MESH
    me = lax.axis_index("space")
    at = pl.program_id(0)
    slots, step, depth, blocks = off_ref.shape
    groups = blocks // GROUP
    half, rhs, _ = own.shape
    quarter = late.shape[0]

    def ahead(source, landing, hops):
        return pltpu.make_async_remote_copy(
            src_ref=source,
            dst_ref=landing,
            send_sem=sent.at[hops - 1],
            recv_sem=got.at[hops - 1],
            device_id={"space": lax.rem(me + hops, count)},
            device_id_type=mesh_ids,
        )

    moves = (ahead(own, following, 1), ahead(late, after, 2))

    @pl.when(at == 0)
    def _():
        barrier = pltpu.get_barrier_semaphore()
        for hops in (1, 2):

            @pl.when(me >= hops)
            def _():
                pl.semaphore_signal(
                    barrier, inc=1, device_id={"space": me - hops}, device_id_type=mesh_ids
                )

        for r in range(rhs):
            turned = x_ref[:, r, :].T
            wide[:, r, :] = jnp.concatenate([turned[:half], turned[half:]], axis=1)
        own[...] = wide[...].astype(jnp.bfloat16)
        low = low_lanes((quarter, rhs, 2 * depth))
        first = pltpu.roll(wide[:quarter], depth, 2)
        late[...] = jnp.where(low, first, wide[quarter:]).astype(jnp.bfloat16)

        @pl.when(me < count - 2)
        def _():
            pl.semaphore_wait(barrier, 2)

        @pl.when(me == count - 2)
        def _():
            pl.semaphore_wait(barrier, 1)

        for hops, move in enumerate(moves, 1):

            @pl.when(me < count - hops)
            def _():
                move.start()

    for pair in range(step // 2):
        for m in range((slots + 1) // 2):
            parts = []
            for row in (2 * pair, 2 * pair + 1):
                first = off_ref[2 * m, row]
                last = 2 * m + 1 == slots
                second = diag_ref[row] if last else off_ref[2 * m + 1, row]
                both = jnp.concatenate([first, second], axis=0).astype(jnp.float32)
                parts.append(both.T.reshape(groups, GROUP, 2 * depth))
            packed = jnp.concatenate(parts, axis=1).astype(jnp.bfloat16)
            out_ref[:, pair * 16 : pair * 16 + 16, m * 2 * depth : (m + 1) * 2 * depth] = packed

    @pl.when(at == pl.num_programs(0) - 1)
    def _():
        own_ref[...] = own[...]
        for hops, (move, landing, out) in enumerate(
            zip(moves, (following, after), (earlier_ref, oldest_ref)), 1
        ):

            @pl.when(me >= hops)
            def _():
                move.wait_recv()
                out[...] = landing[...]

            @pl.when(me < hops)
            def _():
                out[...] = jnp.zeros_like(out)

            @pl.when(me < count - hops)
            def _():
                move.wait_send()


def turn_tiles(count, right_side, off_tiles, diag_tiles):
    slots, rows, depth, blocks = off_tiles.shape
    rhs = right_side.shape[1]
    step = 8
    groups = blocks // GROUP
    half = blocks // 2
    wide = (slots + 1) * depth
    own = jax.ShapeDtypeStruct((half, rhs, 2 * depth), jnp.bfloat16)
    late = jax.ShapeDtypeStruct((half // 2, rhs, 2 * depth), jnp.bfloat16)
    whole = lambda shape: pl.BlockSpec(shape, lambda s: (0,) * len(shape))
    return pl.pallas_call(
        functools.partial(turn_kernel, count),
        grid=(rows // step,),
        in_specs=[
            whole(right_side.shape),
            pl.BlockSpec((slots, step, depth, blocks), lambda s: (0, s, 0, 0)),
            pl.BlockSpec((step, depth, blocks), lambda s: (s, 0, 0)),
        ],
        out_specs=[
            whole(own.shape),
            whole(own.shape),
            whole(late.shape),
            pl.BlockSpec((groups, step * GROUP, wide), lambda s: (0, s, 0)),
        ],
        out_shape=[
            own, own, late, jax.ShapeDtypeStruct((groups, rows * GROUP, wide), jnp.bfloat16)
        ],
        scratch_shapes=[
            pltpu.VMEM(own.shape, jnp.float32),
            pltpu.VMEM(own.shape, jnp.bfloat16),
            pltpu.VMEM(late.shape, jnp.bfloat16),
            pltpu.VMEM(own.shape, jnp.bfloat16),
            pltpu.VMEM(late.shape, jnp.bfloat16),
            pltpu.SemaphoreType.DMA((2,)),
            pltpu.SemaphoreType.DMA((2,)),
        ],
        compiler_params=pltpu.CompilerParams(
            collective_id=1, has_side_effects=True, vmem_limit_bytes=TURN_MIB * 2**20
        ),
        name="turn_tiles",
    )(right_side, off_tiles, diag_tiles)


def main_kernel(
    ids_ref, own_ref, earlier_ref, oldest_ref, t_ref,
    for_oldest_ref, for_earlier_ref, own_out_ref, curve_ref,
    low_table, high_table, low_sum, high_sum, picked, terms,
):
    step = pl.program_id(0)
    half = own_ref.shape[0]
    quarter = oldest_ref.shape[0]
    rhs, lanes = own_ref.shape[1:]
    depth = lanes // 2
    pairs = t_ref.shape[2] // lanes
    starts = (0, 2 * quarter, 2 * quarter + 2 * half)
    base = lax.axis_index("space") * (2 * half) - starts[2]

    def page_of(slot, b):
        block = step * (TOGETHER * GROUP) + b
        return starts[2] + block if slot == 2 * pairs - 1 else ids_ref[slot, block] - base

    @pl.when(step == 0)
    def _():
        low = low_lanes((rhs, lanes))
        for source, start in zip((oldest_ref, earlier_ref, own_ref), starts):
            size = source.shape[0]

            @pl.loop(0, size, unroll=8)
            def _(j):
                page = source[j].astype(jnp.float32)
                other = pltpu.roll(page, depth, 1)
                for table, here in ((low_table, low), (high_table, ~low)):
                    first, second = (page, other) if table is low_table else (other, page)
                    table[start + j] = jnp.where(here, first, 0.0).astype(jnp.bfloat16)
                    table[start + size + j] = jnp.where(here, second, 0.0).astype(jnp.bfloat16)

        @pl.loop(0, low_sum.shape[0], unroll=8)
        def _(j):
            low_sum[j] = jnp.zeros((rhs, lanes), jnp.float32)
            high_sum[j] = jnp.zeros((rhs, lanes), jnp.float32)

        curve_ref[...] = jnp.zeros_like(curve_ref)

    rows = t_ref.shape[1]
    column = lax.broadcasted_iota(jnp.int32, (1, rows), 1) & (GROUP - 1)

    for g in range(TOGETHER):
        for b in range(GROUP):
            for m in range(pairs):
                first, second = page_of(2 * m, g * GROUP + b), page_of(2 * m + 1, g * GROUP + b)
                picked[g, b * rhs : (b + 1) * rhs, m * lanes : (m + 1) * lanes] = (
                    low_table[first] + high_table[second]
                )
    for g in range(TOGETHER):
        image = lax.dot_general(
            picked[g], t_ref[g], (((1,), (1,)), ((), ())), preferred_element_type=jnp.float32
        )
        image = jnp.concatenate(
            [jnp.where(column == c, image[c * rhs : (c + 1) * rhs], 0.0) for c in range(GROUP)],
            axis=0,
        )
        rounded = image.astype(jnp.bfloat16)
        square = image * rounded.astype(jnp.float32)
        curve = curve_ref[...]
        for c in range(GROUP):
            for lane in range(0, rows, lanes):
                curve = curve + square[c * rhs : (c + 1) * rhs, lane : lane + lanes]
        curve_ref[...] = curve
        terms[g] = lax.dot_general(
            rounded, t_ref[g], (((1,), (0,)), ((), ())), preferred_element_type=jnp.float32
        )
    for g in range(TOGETHER):
        for b in range(GROUP):
            for table, odd in ((low_sum, 0), (high_sum, 1)):
                for begin in range(0, pairs, 4):
                    span = range(begin, begin + 4)
                    ids = [page_of(2 * m + odd, g * GROUP + b) for m in span]
                    sums = [
                        table[at]
                        + terms[g, b * rhs : (b + 1) * rhs, m * lanes : (m + 1) * lanes]
                        for at, m in zip(ids, span)
                    ]
                    for at, value in zip(ids, sums):
                        table[at] = value

    @pl.when(step == pl.num_programs(0) - 1)
    def _():
        low = low_lanes((rhs, lanes))

        def total(t):
            mixed = jnp.where(low, low_sum[t], high_sum[t])
            return mixed + pltpu.roll(mixed, depth, 1)

        for out, start in zip((for_oldest_ref, for_earlier_ref, own_out_ref), starts):
            size = out.shape[0]

            @pl.loop(0, size, unroll=8)
            def _(j):
                out[j] = jnp.where(low, total(start + j), total(start + size + j)).astype(out.dtype)


def main_call(ids, own, earlier, oldest, turned):
    half, rhs, lanes = own.shape
    quarter = oldest.shape[0]
    groups, rows, wide = turned.shape
    pages = 4 * half + 2 * quarter
    whole = lambda shape: pl.BlockSpec(shape, lambda s: (0,) * len(shape))
    return pl.pallas_call(
        main_kernel,
        grid=(groups // TOGETHER,),
        in_specs=[
            pl.BlockSpec(memory_space=pltpu.SMEM),
            whole(own.shape),
            whole(earlier.shape),
            whole(oldest.shape),
            pl.BlockSpec((TOGETHER, rows, wide), lambda s: (s, 0, 0)),
        ],
        out_specs=[whole(oldest.shape), whole(own.shape), whole(own.shape), whole((rhs, lanes))],
        out_shape=[
            jax.ShapeDtypeStruct(oldest.shape, jnp.bfloat16),
            jax.ShapeDtypeStruct(own.shape, jnp.bfloat16),
            jax.ShapeDtypeStruct(own.shape, jnp.float32),
            jax.ShapeDtypeStruct((rhs, lanes), jnp.float32),
        ],
        scratch_shapes=[
            pltpu.VMEM((pages, rhs, lanes), jnp.bfloat16),
            pltpu.VMEM((pages, rhs, lanes), jnp.bfloat16),
            pltpu.VMEM((pages, rhs, lanes), jnp.float32),
            pltpu.VMEM((pages, rhs, lanes), jnp.float32),
            pltpu.VMEM((TOGETHER, GROUP * rhs, wide), jnp.bfloat16),
            pltpu.VMEM((TOGETHER, GROUP * rhs, wide), jnp.float32),
        ],
        compiler_params=pltpu.CompilerParams(vmem_limit_bytes=MAIN_MIB * 2**20),
        cost_estimate=pl.CostEstimate(flops=8 * 10**9, bytes_accessed=32 * 2**20, transcendentals=0),
        name="image_and_terms",
    )(ids, own, earlier, oldest, turned)


def finish_kernel(
    count, oldest_ref, earlier_ref, own_ref, curve_ref, x_ref, solution_ref, residual_ref,
    after, following, parts, part, turned, small_sent, small_got, sent, got,
):
    mesh_ids = pl.DeviceIdType.MESH
    me = lax.axis_index("space")
    depth, rhs, blocks = x_ref.shape
    half, _, lanes = own_ref.shape
    quarter = oldest_ref.shape[0]
    row = lax.broadcasted_iota(jnp.int32, (rhs, lanes), 0)
    lane = lax.broadcasted_iota(jnp.int32, (rhs, lanes), 1)
    diagonal = row == lane

    barrier = pltpu.get_barrier_semaphore()

    @pl.loop(1, count)
    def _(k):
        pl.semaphore_signal(
            barrier, inc=1, device_id={"space": lax.rem(me + k, count)}, device_id_type=mesh_ids
        )

    squares = jnp.zeros((rhs, blocks), jnp.float32)
    for k in range(depth):
        squares = squares + x_ref[k] * x_ref[k]
    norms = jnp.sum(squares, axis=1, keepdims=True)
    part[...] = jnp.zeros_like(part)
    part[0:1, :] = jnp.sum(jnp.where(diagonal, norms, 0.0), axis=0, keepdims=True)
    curves = jnp.sum(curve_ref[...], axis=1, keepdims=True)
    part[1:2, :] = jnp.sum(jnp.where(diagonal, curves, 0.0), axis=0, keepdims=True)

    pl.semaphore_wait(barrier, count - 1)

    def small(k, slot):
        return pltpu.make_async_remote_copy(
            src_ref=part,
            dst_ref=parts.at[slot],
            send_sem=small_sent.at[k],
            recv_sem=small_got.at[slot],
            device_id={"space": lax.rem(me + k, count)},
            device_id_type=mesh_ids,
        )

    @pl.loop(1, count)
    def _(k):
        small(k, me).start()

    def behind(source, landing, steps):
        return pltpu.make_async_remote_copy(
            src_ref=source,
            dst_ref=landing,
            send_sem=sent.at[steps - 1],
            recv_sem=got.at[steps - 1],
            device_id={"space": lax.rem(me + count - steps, count)},
            device_id_type=mesh_ids,
        )

    moves = (behind(earlier_ref, following, 1), behind(oldest_ref, after, 2))
    for steps, move in enumerate(moves, 1):

        @pl.when(me >= steps)
        def _():
            move.start()

    parts[me] = part[...]

    @pl.loop(1, count)
    def _(k):
        small(k, lax.rem(me + k, count)).wait_recv()

    total = parts[0]
    for slot in range(1, count):
        total = total + parts[slot]
    ratio = total[0:1, :] / total[1:2, :]
    scale = jnp.sum(jnp.where(diagonal, ratio, 0.0), axis=1, keepdims=True)
    for k in range(depth):
        solution_ref[k] = scale * x_ref[k]

    for steps, (move, landing) in enumerate(zip(moves, (following, after)), 1):

        @pl.when(me < count - steps)
        def _():
            move.wait_recv()

        @pl.when(me >= count - steps)
        def _():
            landing[...] = jnp.zeros_like(landing)

    low = low_lanes((rhs, lanes))
    for j in range(quarter):
        page = after[j].astype(jnp.float32)
        own_ref_low = jnp.where(low, 0.0, pltpu.roll(page, depth, 1))
        turned[j] = own_ref[j] + following[j].astype(jnp.float32) + own_ref_low
        at = quarter + j
        turned[at] = own_ref[at] + following[at].astype(jnp.float32) + jnp.where(low, 0.0, page)
    for r in range(rhs):
        side = turned[:, r, :].T
        side = jnp.concatenate([side[:depth], side[depth:]], axis=1)
        residual_ref[:, r, :] = x_ref[:, r, :] - scale[r : r + 1] * side

    @pl.loop(1, count)
    def _(k):
        small(k, me).wait_send()

    for steps, move in enumerate(moves, 1):

        @pl.when(me >= steps)
        def _():
            move.wait_send()


def finish(count, for_oldest, for_earlier, own_sum, curve_parts, right_side):
    vmem = pl.BlockSpec(memory_space=pltpu.VMEM)
    return pl.pallas_call(
        functools.partial(finish_kernel, count),
        in_specs=[vmem] * 5,
        out_specs=[vmem] * 2,
        out_shape=[jax.ShapeDtypeStruct(right_side.shape, jnp.float32)] * 2,
        scratch_shapes=[
            pltpu.VMEM(for_oldest.shape, jnp.bfloat16),
            pltpu.VMEM(for_earlier.shape, jnp.bfloat16),
            pltpu.VMEM((count, 8, own_sum.shape[2]), jnp.float32),
            pltpu.VMEM((8, own_sum.shape[2]), jnp.float32),
            pltpu.VMEM(own_sum.shape, jnp.float32),
            pltpu.SemaphoreType.DMA((count,)),
            pltpu.SemaphoreType.DMA((count,)),
            pltpu.SemaphoreType.DMA((2,)),
            pltpu.SemaphoreType.DMA((2,)),
        ],
        compiler_params=pltpu.CompilerParams(
            collective_id=0, has_side_effects=True, vmem_limit_bytes=24 * 2**20
        ),
        name="finish",
    )(for_oldest, for_earlier, own_sum, curve_parts, right_side)


def on_device(count, right_side, diag_tiles, off_tiles, neighbours):
    own, earlier, oldest, turned = turn_tiles(count, right_side, off_tiles, diag_tiles)
    for_oldest, for_earlier, own_sum, curve_parts = main_call(neighbours, own, earlier, oldest, turned)
    return tuple(finish(count, for_oldest, for_earlier, own_sum, curve_parts, right_side))


def solution(mesh):
    placed = (
        P(None, None, ("grp", "space")),
        P(None, None, ("grp", "space")),
        P(None, None, None, ("grp", "space")),
        P(None, ("grp", "space")),
    )
    return jax.shard_map(
        functools.partial(on_device, mesh.shape["space"]),
        mesh=mesh,
        in_specs=placed,
        out_specs=(P(None, None, ("grp", "space")), P(None, None, ("grp", "space"))),
        check_vma=False,
    )
```
